32 devices in a mesh: groups: 2 (over x), bl: 16 (over z, y, core).
Axes of the slice: x: 2, y: 2, z: 4, core: 2. Of those that a mesh axis runs over, the one named last changes fastest.
Arguments:
- grid: bfloat16 [32, 1024, 2048], P(('groups', 'bl')), parts along dimension 0, may hold values from -6 to 6
- patch_owner: int32 [4096, 1], P(('groups', 'bl')), parts along dimension 0, may hold values from 0 to 15; in each aligned block of 128 rows (0 to 127, 128 to 255, ...) at most 12 rows name the same one
- patch_column: int32 [4096], P(('groups', 'bl')), parts along dimension 0, may hold values from 0 to 1023
- aperture_index: int32 [4096], P(('groups', 'bl')), parts along dimension 0, may hold values from 0 to 7
- w_index: int32 [4096, 8], P(('groups', 'bl')), parts along dimension 0, may hold values from 0 to 31
- a_kernels: float32 [8, 2, 1024], replicated, may hold values from -6 to 6
- w_kernels: float32 [32, 2, 1024], replicated, may hold values from -6 to 6
- channel_response: bfloat16 [2, 1024, 128], P(None, None, 'groups'), parts along dimension 2, may hold values from -0.125 to 0.125
- time_owner: int32 [4096, 1], P(('groups', 'bl')), parts along dimension 0, may hold values from 0 to 15; in each aligned block of 128 rows (0 to 127, 128 to 255, ...) at most 12 rows name the same one
- observed: bfloat16 [6144, 1024], P(('groups', 'bl')), parts along dimension 0, may hold values from -6 to 6
Outputs:
- residual: bfloat16 [6144, 1024], P(('groups', 'bl')), parts along dimension 0
The draws below stay inside these ranges and needn't reach their ends.
There are 2 independent parts, one for each index of `groups`. The reference program is written for one: setup_inputs(seed, part) draws one part's arguments, and reference() takes and returns one part's arrays. A program takes and returns all parts, laid end to end along the dimension named above; an argument that names none is the same for every part. Nothing has to cross between parts.
Inputs may be any that keep to these rules, and one draw needn't show every extreme that they name: `patch_owner`: within the rows of one device no owner is named by more than 12 rows, a bound that some block reaches. `time_owner`: within the rows of one device no owner is named by more than 12 rows, a bound that some block reaches.
All inputs are finite; a program needn't handle non-finite values.
Results may differ from the reference program's by a relative error of at most 0.0052.
Values may be sent and summed in bfloat16 or wider, within the bound.
A program may use at most 64 MiB of HBM per device.

```python
import math
import jax
import jax.numpy as jnp
import numpy as np
from jax import lax

SUPPORT = 32
CH = 64
TS = 8
W_PLANES = 32
A_KERNELS = 8
ROWS_DEV = 128
CAP = 12
ROWS = 2048
PATCH_DEV = 1024
N_BL = 16


def touch_ends(drawn, stream_key, smallest, high):
    longest = drawn.shape.index(max(drawn.shape))
    spots = []
    for shift in (0, 1):
        where = [jax.random.randint(jax.random.fold_in(stream_key, axis), (), 0, length) for axis, length in enumerate(drawn.shape)]
        where[longest] = (where[longest] + shift) % drawn.shape[longest]
        spots.append(tuple(where))
    return drawn.at[spots[0]].set(smallest).at[spots[1]].set(high)


def block_scale(key, shape, split, least, largest):
    loudness, own = 1.0, jax.random.fold_in(key, 6)
    for axis_at, parts in split:
        steps = jnp.exp(jax.random.uniform(jax.random.fold_in(own, axis_at), (parts,), jnp.float32, least / len(split), largest / len(split)))
        loudness = loudness * jnp.repeat(steps, shape[axis_at] // parts).reshape([-1 if axis == axis_at else 1 for axis in range(len(shape))])
    return loudness


def routed_block(rng, own, number, rows, number_of, top, most, slope):
    sequence = jax.random.permutation(rng, number_of)
    heavy_load, ordinary = portions_of(number_of, rows * top, most, slope, True), portions_of(number_of, rows * top, most, slope, False)
    places = jnp.arange(number_of)

    def named(lengths, offset_by):
        used = int((lengths > 0).sum())
        fixed = max(1, used // 4)
        passed = fixed + (places - fixed + offset_by * (used - fixed)) % max(1, number_of - fixed)
        return jnp.zeros((number_of,), jnp.int32).at[sequence[jnp.where(places < fixed, places, passed)]].set(jnp.asarray(lengths, jnp.int32))

    lengths = jnp.where(number % 4 == 0, named(heavy_load, number // 4), named(ordinary, number - number // 4 - 1))
    mixed = jax.random.permutation(jax.random.fold_in(own, 3), number_of)
    giver, receiver = mixed[0:number_of // 2 * 2:2], mixed[1:number_of // 2 * 2:2]
    slack = jnp.minimum(lengths[giver] - 1, most - lengths[receiver]) // 2
    slack = jnp.where((giver == sequence[0]) | (receiver == sequence[0]) | (lengths[receiver] == 0), 0, jnp.maximum(slack, 0))
    passed = jax.random.randint(jax.random.fold_in(own, 4), (number_of // 2,), 0, 1 << 20) % (slack + 1)
    lengths = lengths.at[giver].add(-passed).at[receiver].add(passed)
    labels = jnp.searchsorted(jnp.cumsum(lengths), jnp.arange(rows * top), side="right").astype(jnp.int32)
    table = labels.reshape(top, rows).T
    table = table[jax.random.permutation(jax.random.fold_in(own, 1), rows)]
    offset_by = jax.random.randint(jax.random.fold_in(own, 2), (rows, 1), 0, top)
    return jnp.take_along_axis(table, (jnp.arange(top)[None, :] + offset_by) % top, axis=1)


def portions_of(number_of, total, most, lean, full):
    portions = [(1 << 20) // math.isqrt(rank ** lean) + 1 for rank in range(1, number_of + 1)]
    largest = most if full else min(most, max(-(-total // number_of), total * portions[0] // sum(portions)))
    least = 1 if total - largest >= number_of - 1 else 0
    holding, rest = [largest] + [least] * (number_of - 1), total - largest - least * (number_of - 1)
    while rest > 0:
        candidates = [i for i in range(1, number_of) if holding[i] < largest] or [i for i in range(1, number_of) if holding[i] < most]
        whole, left = sum([portions[i] for i in candidates]), rest
        for i in candidates:
            addition = min(most - holding[i], max(1, left * portions[i] // whole), rest)
            holding[i] = holding[i] + addition
            rest = rest - addition
    return np.array(holding)


def normal_values(stream_key, extent, spread, bound, pieces=(), kind=jnp.bfloat16):
    array = jax.random.normal(stream_key, extent, jnp.float32) * spread
    if len(pieces) > 0:
        array = block_scale(stream_key, extent, pieces, -0.22, 0.18) * array
    return jnp.clip(array, min=-bound, max=bound).astype(kind)


def setup_inputs(seed: int = 0, part: int = 0) -> dict:
    key_of = jax.random.split(jax.random.key(seed), 11)
    own_keys = jax.random.split(jax.random.fold_in(key_of[10], part), 11)
    grid = normal_values(own_keys[0], (N_BL, PATCH_DEV, 2 * SUPPORT * SUPPORT), 1.0, 6.0, ((0, 16),))
    patch_owner_keys = jax.random.split(jax.random.fold_in(own_keys[1], 1), ROWS // ROWS_DEV)
    patch_owner_turns = jax.random.permutation(jax.random.fold_in(own_keys[1], 3), ROWS // ROWS_DEV)
    patch_owner = jax.vmap(lambda own, number: routed_block(jax.random.fold_in(own_keys[1], 2), own, number, ROWS_DEV, N_BL, 1, CAP, 2))(patch_owner_keys, patch_owner_turns).reshape((ROWS, 1))
    patch_column = touch_ends(jax.random.randint(own_keys[2], (ROWS,), 0, PATCH_DEV), jax.random.fold_in(own_keys[2], 1), 0, PATCH_DEV - 1).astype(jnp.int32)
    aperture_index = touch_ends(jax.random.randint(own_keys[3], (ROWS,), 0, A_KERNELS), jax.random.fold_in(own_keys[3], 1), 0, A_KERNELS - 1).astype(jnp.int32)
    w_index = touch_ends(jax.random.randint(own_keys[4], (ROWS, TS), 0, W_PLANES), jax.random.fold_in(own_keys[4], 1), 0, W_PLANES - 1).astype(jnp.int32)
    a_kernels = normal_values(key_of[5], (A_KERNELS, 2, SUPPORT * SUPPORT), 0.7071, 6.0, (), jnp.float32)
    w_kernels = normal_values(key_of[6], (W_PLANES, 2, SUPPORT * SUPPORT), 1.0, 6.0, (), jnp.float32)
    channel_response = normal_values(own_keys[7], (2, SUPPORT * SUPPORT, CH), (2 * SUPPORT * SUPPORT) ** -0.5, 0.125)
    time_owner_keys = jax.random.split(jax.random.fold_in(own_keys[8], 1), ROWS // ROWS_DEV)
    time_owner_turns = jax.random.permutation(jax.random.fold_in(own_keys[8], 3), ROWS // ROWS_DEV)
    time_owner = jax.vmap(lambda own, number: routed_block(jax.random.fold_in(own_keys[8], 2), own, number, ROWS_DEV, N_BL, 1, CAP, 2))(time_owner_keys, time_owner_turns).reshape((ROWS, 1))
    observed = normal_values(own_keys[9], (N_BL * N_BL * CAP, TS * 2 * CH), 1.0, 6.0, ((0, 16),))
    return dict(grid=grid, patch_owner=patch_owner, patch_column=patch_column, aperture_index=aperture_index, w_index=w_index, a_kernels=a_kernels, w_kernels=w_kernels, channel_response=channel_response, time_owner=time_owner, observed=observed)


def slot_of(owner_column, peer_count, capacity):
    owners = owner_column[:, 0]
    hits = (owners[:, None] == jnp.arange(peer_count, dtype=jnp.int32)[None, :]).astype(jnp.int32)
    before = jnp.cumsum(hits, axis=0) - hits
    ranks = jnp.sum(before * hits, axis=1)
    return (owners * capacity + ranks).astype(jnp.int32)


def complex_times(first_factor, second_factor):
    real_part = first_factor[..., 0, :] * second_factor[..., 0, :] - first_factor[..., 1, :] * second_factor[..., 1, :]
    imag_part = first_factor[..., 0, :] * second_factor[..., 1, :] + first_factor[..., 1, :] * second_factor[..., 0, :]
    return jnp.stack([real_part, imag_part], axis=-2)


def response_matrix(channel_response):
    real_part = channel_response[0]
    imag_part = channel_response[1]
    upper_half = jnp.concatenate([real_part, imag_part], axis=1)
    lower_half = jnp.concatenate([-imag_part, real_part], axis=1)
    return jnp.concatenate([upper_half, lower_half], axis=0)


def predict(patches, aperture, wplanes, a_kernels, w_kernels, matrix):
    row_count = patches.shape[0]
    tapered = complex_times(patches.astype(jnp.float32).reshape(row_count, 2, -1), jnp.take(a_kernels, aperture, axis=0))
    outputs = []
    for sample in range(wplanes.shape[1]):
        screen = jnp.take(w_kernels, wplanes[:, sample], axis=0)
        weighted = complex_times(tapered, screen).reshape(row_count, -1).astype(jnp.bfloat16)
        outputs.append(jnp.dot(weighted, matrix, preferred_element_type=jnp.float32))
    return jnp.concatenate(outputs, axis=1).astype(jnp.bfloat16)


def reference(grid, patch_owner, patch_column, aperture_index, w_index, a_kernels, w_kernels, channel_response, time_owner, observed):
    matrix = response_matrix(channel_response)

    def one_block(row_block):
        owners, columns, aperture, wplanes = row_block
        patches = grid[owners, columns]
        return predict(patches, aperture, wplanes, a_kernels, w_kernels, matrix)

    visibilities = lax.map(one_block, (patch_owner.reshape(N_BL, ROWS_DEV), patch_column.reshape(N_BL, ROWS_DEV),
                                       aperture_index.reshape(N_BL, ROWS_DEV), w_index.reshape(N_BL, ROWS_DEV, TS)))
    time_rows = time_owner.reshape(N_BL, ROWS_DEV, 1)
    local_slots = jax.vmap(lambda owner_rows: slot_of(owner_rows, N_BL, CAP))(time_rows)
    owners = time_rows[:, :, 0]
    ranks = local_slots - owners * CAP
    sources = jnp.arange(N_BL, dtype=jnp.int32)[:, None]
    targets = (owners * (N_BL * CAP) + sources * CAP + ranks).astype(jnp.int32)
    updated = observed.astype(jnp.float32).at[targets.reshape(-1)].add(
        -visibilities.reshape(-1, TS * 2 * CH).astype(jnp.float32))
    return updated.astype(jnp.bfloat16)
```

```python
import functools

import jax
import jax.numpy as jnp
from jax import lax
from jax.experimental import pallas as pl
from jax.experimental.pallas import tpu as pltpu
from jax.sharding import PartitionSpec as P

F32 = jnp.float32
BF16 = jnp.bfloat16
LANES = 128


def iota(shape, axis):
    return lax.broadcasted_iota(jnp.int32, shape, axis)


def dot(a, b):
    return jnp.dot(a, b, preferred_element_type=F32)


def dot_nt(a, b):
    return lax.dot_general(a, b, (((1,), (1,)), ((), ())), preferred_element_type=F32)


def owner_and_rank(owner, n):
    rows = owner.shape[1]
    hits = (iota((n, rows), 0) == owner).astype(F32)
    earlier = (iota((rows, rows), 0) < iota((rows, rows), 1)).astype(F32).astype(BF16)
    before = dot(hits.astype(BF16), earlier)
    return owner, jnp.sum(before * hits, axis=0, keepdims=True).astype(jnp.int32)


def one_hot_rows(slot, count):
    return (iota((count, slot.shape[1]), 0) == slot).astype(F32).astype(BF16)


def kernel(
    n, cap, capp, ts, block,
    meta_ref, grid_hbm, a_ref, w_ref, chan_ref, obs_hbm,
    out_ref,
    grid, obs, rs, rq, acat, wcat, mat, tap, wt, sbuf, rbuf, wide, xbuf, sbuf2, rbuf2,
    local_sem, send_sem, req_sem, pred_sem, time_sem,
):
    me = lax.axis_index("bl")
    rows = meta_ref.shape[1]
    cells = grid.shape[1] // 2
    columns = grid.shape[0]
    span = cap * ts

    load_grid = pltpu.make_async_copy(grid_hbm, grid, local_sem.at[0])
    load_obs = pltpu.make_async_copy(obs_hbm, obs, local_sem.at[1])
    load_grid.start()
    load_obs.start()

    barrier = pltpu.get_barrier_semaphore()

    def greet(i, carry):
        pl.semaphore_signal(barrier, inc=1, device_id={"bl": lax.rem(me + i, n)},
                            device_id_type=pl.DeviceIdType.MESH)
        return carry

    lax.fori_loop(1, n, greet, 0)

    meta = meta_ref[...]
    p_owner, p_rank = owner_and_rank(meta[11:12], n)
    t_owner, t_rank = owner_and_rank(meta[12:13], n)
    data = jnp.concatenate([meta.astype(F32), jnp.zeros((LANES - 16, rows), F32)], axis=0).astype(BF16)
    wanted = dot_nt(one_hot_rows(p_owner * capp + p_rank, n * capp), data)
    rs[...] = wanted.reshape(n, capp, LANES)

    pl.semaphore_wait(barrier, n - 1)

    def request(i):
        peer = lax.rem(me + i, n)
        return pltpu.make_async_remote_copy(
            src_ref=rs.at[peer], dst_ref=rq.at[me], send_sem=send_sem.at[0, i], recv_sem=req_sem.at[me],
            device_id={"bl": peer}, device_id_type=pl.DeviceIdType.MESH)

    def predicted(i):
        peer = lax.rem(me + i, n)
        return pltpu.make_async_remote_copy(
            src_ref=sbuf.at[i - 1], dst_ref=rbuf.at[me], send_sem=send_sem.at[1, i], recv_sem=pred_sem.at[me],
            device_id={"bl": peer}, device_id_type=pl.DeviceIdType.MESH)

    def timed(i):
        peer = lax.rem(me + i, n)
        return pltpu.make_async_remote_copy(
            src_ref=sbuf2.at[peer], dst_ref=rbuf2.at[me], send_sem=send_sem.at[2, i], recv_sem=time_sem.at[me],
            device_id={"bl": peer}, device_id_type=pl.DeviceIdType.MESH)

    def arrival(buf, sem, i):
        sender = lax.rem(me + i, n)
        return pltpu.make_async_copy(buf.at[sender], buf.at[sender], sem.at[sender])

    def each(low, high, act):
        def step(i, carry):
            act(i)
            return carry
        lax.fori_loop(low, high, step, 0)

    each(1, n, lambda i: request(i).start())
    rq[me] = rs[me]

    for part in range(2):
        at = pl.ds(part * cells, cells)
        for source, table in ((a_ref, acat), (w_ref, wcat)):
            count = source.shape[0]
            value = source[:, part, :]
            high = value.astype(BF16)
            table[0:count, at] = high
            table[count:2 * count, at] = (value - high.astype(F32)).astype(BF16)
    ch = chan_ref.shape[2]
    left = (iota((ch, 2 * ch), 1) == iota((ch, 2 * ch), 0)).astype(F32).astype(BF16)
    right = (iota((ch, 2 * ch), 1) == iota((ch, 2 * ch), 0) + ch).astype(F32).astype(BF16)
    real, imag = chan_ref[0], chan_ref[1]
    mat[0:cells] = (dot(real, left) + dot(imag, right)).astype(BF16)
    mat[cells:2 * cells] = (dot(real, right) - dot(imag, left)).astype(BF16)
    move = dot_nt(one_hot_rows(t_owner * cap + t_rank, n * cap),
                  one_hot_rows(p_owner * cap + p_rank, n * cap)).astype(BF16)

    load_grid.wait()
    each(1, n, lambda i: arrival(rq, req_sem, i).wait())

    n_a = a_ref.shape[0]
    peers = min(n, 256 // capp)
    wide_step = 256

    def taper(b, carry):
        lot = peers * capp
        req = rq[pl.ds(b * peers, peers)].reshape(lot, LANES)
        column = req[:, 0:1] * 32.0 + req[:, 1:2]
        pick = (iota((lot, columns), 1).astype(F32) == column).astype(F32).astype(BF16)
        lane = iota((lot, 2 * n_a), 1)
        lane = jnp.where(lane >= n_a, lane - n_a, lane)
        a_pick = (lane.astype(F32) == req[:, 2:3]).astype(F32).astype(BF16)
        for start in range(0, cells, wide_step):
            re, im = pl.ds(start, wide_step), pl.ds(cells + start, wide_step)
            p_re, p_im = dot(pick, grid[:, re]), dot(pick, grid[:, im])
            a_re, a_im = dot(a_pick, acat[:, re]), dot(a_pick, acat[:, im])
            tap[pl.ds(b * peers, peers), :, re] = (p_re * a_re - p_im * a_im).reshape(peers, capp, wide_step)
            tap[pl.ds(b * peers, peers), :, im] = (p_re * a_im + p_im * a_re).reshape(peers, capp, wide_step)
        return carry

    lax.fori_loop(0, n // peers, taper, 0)

    n_w = w_ref.shape[0]

    def spread(value):
        return jnp.broadcast_to(value[:, None, :], (cap, ts, value.shape[1])).reshape(span, value.shape[1])

    def predict(c, carry):
        picks = []
        for j in range(block):
            req = spread(rq[lax.rem(me + c * block + j + 1, n), 0:cap, :])
            sample = iota((span, LANES), 0)
            mine = iota((span, LANES), 1) == 3 + jnp.bitwise_and(sample, ts - 1)
            plane = jnp.sum(jnp.where(mine, req, 0.0), axis=1, keepdims=True)
            lane = iota((span, 2 * n_w), 1)
            lane = jnp.where(lane >= n_w, lane - n_w, lane)
            picks.append((lane.astype(F32) == plane).astype(F32))
        w_pick = jnp.concatenate(picks, axis=0).astype(BF16)
        for start in range(0, cells, wide_step):
            re, im = pl.ds(start, wide_step), pl.ds(cells + start, wide_step)
            s_re, s_im = dot(w_pick, wcat[:, re]), dot(w_pick, wcat[:, im])
            for j in range(block):
                p = lax.rem(me + c * block + j + 1, n)
                t_re, t_im = spread(tap[p, 0:cap, re]), spread(tap[p, 0:cap, im])
                w_re, w_im = s_re[j * span:(j + 1) * span], s_im[j * span:(j + 1) * span]
                wt[pl.ds(j * span, span), re] = (t_re * w_re - t_im * w_im).astype(BF16)
                wt[pl.ds(j * span, span), im] = (t_re * w_im + t_im * w_re).astype(BF16)
        result = dot(wt[...], mat[...]).astype(BF16)
        sbuf[pl.ds(c * block, block)] = result.reshape(block, span, LANES)
        for j in range(block):
            i = c * block + j + 1

            @pl.when(i < n)
            def _():
                predicted(i).start()
        return carry

    lax.fori_loop(0, n // block, predict, 0)
    rbuf[me] = sbuf[n - 1]
    each(1, n, lambda i: arrival(rbuf, pred_sem, i).wait())

    total = n * cap
    wide[...] = rbuf[...].reshape(n * span, LANES).astype(F32)
    for t in range(ts):
        xbuf[:, pl.ds(t * LANES, LANES)] = wide[pl.ds(t, total, stride=ts), :].astype(BF16)
    moved = dot(move, xbuf[...])
    for t in range(ts):
        wide[pl.ds(t, total, stride=ts), :] = moved[:, t * LANES:(t + 1) * LANES]
    sbuf2[...] = wide[...].astype(BF16).reshape(n, span, LANES)
    each(1, n, lambda i: timed(i).start())
    rbuf2[me] = sbuf2[me]
    load_obs.wait()
    each(1, n, lambda i: arrival(rbuf2, time_sem, i).wait())

    wide[...] = rbuf2[...].reshape(n * span, LANES).astype(F32)
    for t in range(ts):
        at = pl.ds(t * LANES, LANES)
        out_ref[:, at] = (obs[:, at].astype(F32) - wide[pl.ds(t, total, stride=ts), :]).astype(BF16)

    def sent(i):
        request(i).wait_send()
        predicted(i).wait_send()
        timed(i).wait_send()

    each(1, n, sent)


def local(
    grid,
    patch_owner,
    patch_column,
    aperture_index,
    w_index,
    a_kernels,
    w_kernels,
    channel_response,
    time_owner,
    observed,
):
    n = lax.axis_size("bl")
    cap = observed.shape[0] // n
    capp = -(-cap // 8) * 8
    rows, ts = w_index.shape
    columns, width = grid.shape[1:]
    n_a, n_w = a_kernels.shape[0], w_kernels.shape[0]
    block = 4
    span = cap * ts
    meta = jnp.concatenate(
        [(patch_column >> 5)[None], (patch_column & 31)[None], aperture_index[None], w_index.T,
         patch_owner.T, time_owner.T, jnp.zeros((3, rows), jnp.int32)], axis=0)
    vmem = pl.BlockSpec(memory_space=pltpu.VMEM)
    hbm = pl.BlockSpec(memory_space=pl.ANY)
    return pl.pallas_call(
        functools.partial(kernel, n, cap, capp, ts, block),
        out_shape=jax.ShapeDtypeStruct(observed.shape, BF16),
        in_specs=[vmem, hbm, vmem, vmem, vmem, hbm],
        out_specs=vmem,
        scratch_shapes=[
            pltpu.VMEM((columns, width), BF16),
            pltpu.VMEM(observed.shape, BF16),
            pltpu.VMEM((n, capp, LANES), F32),
            pltpu.VMEM((n, capp, LANES), F32),
            pltpu.VMEM((2 * n_a, width), BF16),
            pltpu.VMEM((2 * n_w, width), BF16),
            pltpu.VMEM((width, 2 * channel_response.shape[2]), BF16),
            pltpu.VMEM((n, capp, width), F32),
            pltpu.VMEM((block * span, width), BF16),
            pltpu.VMEM((n, span, LANES), BF16),
            pltpu.VMEM((n, span, LANES), BF16),
            pltpu.VMEM((n * span, LANES), F32),
            pltpu.VMEM((n * cap, ts * LANES), BF16),
            pltpu.VMEM((n, span, LANES), BF16),
            pltpu.VMEM((n, span, LANES), BF16),
            pltpu.SemaphoreType.DMA((2,)),
            pltpu.SemaphoreType.DMA((3, n)),
            pltpu.SemaphoreType.DMA((n,)),
            pltpu.SemaphoreType.DMA((n,)),
            pltpu.SemaphoreType.DMA((n,)),
        ],
        compiler_params=pltpu.CompilerParams(
            collective_id=0, has_side_effects=True, vmem_limit_bytes=48 * 1024 * 1024),
    )(meta, grid.reshape(columns, width), a_kernels, w_kernels, channel_response, observed)


def solution(mesh):
    in_specs = (
        P(("groups", "bl"), None, None),
        P(("groups", "bl"), None),
        P(("groups", "bl")),
        P(("groups", "bl")),
        P(("groups", "bl"), None),
        P(),
        P(),
        P(None, None, "groups"),
        P(("groups", "bl"), None),
        P(("groups", "bl"), None),
    )
    out_specs = P(("groups", "bl"), None)
    return jax.shard_map(local, mesh=mesh, in_specs=in_specs, out_specs=out_specs, check_vma=False)
```

```python
import functools

import jax
import jax.numpy as jnp
from jax import lax
from jax.experimental import pallas as pl
from jax.experimental.pallas import tpu as pltpu
from jax.sharding import PartitionSpec as P

F32 = jnp.float32
BF16 = jnp.bfloat16
LANES = 128


def iota(shape, axis):
    return lax.broadcasted_iota(jnp.int32, shape, axis)


def dot(a, b):
    return jnp.dot(a, b, preferred_element_type=F32)


def dot_nt(a, b):
    return lax.dot_general(a, b, (((1,), (1,)), ((), ())), preferred_element_type=F32)


def owner_and_rank(owner, n):
    rows = owner.shape[1]
    hits = (iota((n, rows), 0) == owner).astype(F32)
    earlier = (iota((rows, rows), 0) < iota((rows, rows), 1)).astype(F32).astype(BF16)
    before = dot(hits.astype(BF16), earlier)
    return owner, jnp.sum(before * hits, axis=0, keepdims=True).astype(jnp.int32)


def one_hot_rows(slot, count):
    return (iota((count, slot.shape[1]), 0) == slot).astype(F32).astype(BF16)


def kernel(
    n, cap, capp, ts, block,
    grid_hbm, powner_hbm, pcol_hbm, aper_hbm, windex_hbm, a_hbm, w_hbm, chan_hbm, towner_hbm, obs_hbm,
    out_ref,
    grid, powner, pcol, aper, windex, a_ref, w_ref, chan_ref, towner, obs, rs, rq, acat, wcat, mat, tap, wt, sbuf, rbuf, wide, xbuf, sbuf2, rbuf2,
    local_sem, send_sem, req_sem, pred_sem, time_sem,
):
    me = lax.axis_index("bl")
    rows = windex.shape[1]
    cells = grid.shape[1] // 2
    columns = grid.shape[0]
    span = cap * ts

    pairs = [(powner_hbm, powner), (pcol_hbm, pcol), (aper_hbm, aper), (windex_hbm, windex), (towner_hbm, towner),
             (a_hbm, a_ref), (w_hbm, w_ref), (chan_hbm, chan_ref), (grid_hbm, grid), (obs_hbm, obs)]
    loads = [pltpu.make_async_copy(source, target, local_sem.at[k]) for k, (source, target) in enumerate(pairs)]
    for load in loads:
        load.start()

    barrier = pltpu.get_barrier_semaphore()

    def greet(i, carry):
        pl.semaphore_signal(barrier, inc=1, device_id={"bl": lax.rem(me + i, n)},
                            device_id_type=pl.DeviceIdType.MESH)
        return carry

    lax.fori_loop(1, n, greet, 0)

    for load in loads[:5]:
        load.wait()
    p_owner, p_rank = owner_and_rank(powner[...], n)
    t_owner, t_rank = owner_and_rank(towner[...], n)
    column = pcol[...]
    place = iota((8, rows), 0)
    head = jnp.where(place == 0, jnp.right_shift(column, 5),
                     jnp.where(place == 1, jnp.bitwise_and(column, 31), jnp.where(place == 2, aper[...], 0)))
    data = jnp.concatenate([head.astype(F32), windex[...].astype(F32), jnp.zeros((LANES - 8 - ts, rows), F32)],
                           axis=0).astype(BF16)
    wanted = dot_nt(one_hot_rows(p_owner * capp + p_rank, n * capp), data)
    rs[...] = wanted.reshape(n, capp, LANES)

    pl.semaphore_wait(barrier, n - 1)

    def request(i):
        peer = lax.rem(me + i, n)
        return pltpu.make_async_remote_copy(
            src_ref=rs.at[peer], dst_ref=rq.at[me], send_sem=send_sem.at[0, i], recv_sem=req_sem.at[me],
            device_id={"bl": peer}, device_id_type=pl.DeviceIdType.MESH)

    def predicted(i):
        peer = lax.rem(me + i, n)
        return pltpu.make_async_remote_copy(
            src_ref=sbuf.at[i - 1], dst_ref=rbuf.at[me], send_sem=send_sem.at[1, i], recv_sem=pred_sem.at[me],
            device_id={"bl": peer}, device_id_type=pl.DeviceIdType.MESH)

    def timed(i):
        peer = lax.rem(me + i, n)
        return pltpu.make_async_remote_copy(
            src_ref=sbuf2.at[peer], dst_ref=rbuf2.at[me], send_sem=send_sem.at[2, i], recv_sem=time_sem.at[me],
            device_id={"bl": peer}, device_id_type=pl.DeviceIdType.MESH)

    def arrival(buf, sem, i):
        sender = lax.rem(me + i, n)
        return pltpu.make_async_copy(buf.at[sender], buf.at[sender], sem.at[sender])

    def each(low, high, act):
        def step(i, carry):
            act(i)
            return carry
        lax.fori_loop(low, high, step, 0)

    each(1, n, lambda i: request(i).start())
    rq[me] = rs[me]

    for load in loads[5:8]:
        load.wait()
    for part in range(2):
        at = pl.ds(part * cells, cells)
        for source, table in ((a_ref, acat), (w_ref, wcat)):
            count = source.shape[0]
            value = source[:, part, :]
            high = value.astype(BF16)
            table[0:count, at] = high
            table[count:2 * count, at] = (value - high.astype(F32)).astype(BF16)
    real, imag = chan_ref[0], chan_ref[1]
    mat[0:cells] = jnp.concatenate([real, imag], axis=0).T
    mat[cells:2 * cells] = jnp.concatenate([-imag, real], axis=0).T
    move = dot_nt(one_hot_rows(t_owner * cap + t_rank, n * cap),
                  one_hot_rows(p_owner * cap + p_rank, n * cap)).astype(BF16)

    loads[8].wait()
    each(1, n, lambda i: arrival(rq, req_sem, i).wait())

    n_a = a_ref.shape[0]
    peers = min(n, 256 // capp)
    wide_step = 256

    def taper(b, carry):
        lot = peers * capp
        req = rq[pl.ds(b * peers, peers)].reshape(lot, LANES)
        column = req[:, 0:1] * 32.0 + req[:, 1:2]
        pick = (iota((lot, columns), 1).astype(F32) == column).astype(F32).astype(BF16)
        lane = iota((lot, 2 * n_a), 1)
        lane = jnp.where(lane >= n_a, lane - n_a, lane)
        a_pick = (lane.astype(F32) == req[:, 2:3]).astype(F32).astype(BF16)
        for start in range(0, cells, wide_step):
            re, im = pl.ds(start, wide_step), pl.ds(cells + start, wide_step)
            p_re, p_im = dot(pick, grid[:, re]), dot(pick, grid[:, im])
            a_re, a_im = dot(a_pick, acat[:, re]), dot(a_pick, acat[:, im])
            tap[pl.ds(b * peers, peers), :, re] = (p_re * a_re - p_im * a_im).reshape(peers, capp, wide_step)
            tap[pl.ds(b * peers, peers), :, im] = (p_re * a_im + p_im * a_re).reshape(peers, capp, wide_step)
        return carry

    lax.fori_loop(0, n // peers, taper, 0)

    n_w = w_ref.shape[0]

    def spread(value):
        return jnp.broadcast_to(value[:, None, :], (cap, ts, value.shape[1])).reshape(span, value.shape[1])

    def predict(c, carry):
        picks = []
        for j in range(block):
            req = spread(rq[lax.rem(me + c * block + j + 1, n), 0:cap, :])
            sample = iota((span, LANES), 0)
            mine = iota((span, LANES), 1) == 8 + jnp.bitwise_and(sample, ts - 1)
            plane = jnp.sum(jnp.where(mine, req, 0.0), axis=1, keepdims=True)
            lane = iota((span, 2 * n_w), 1)
            lane = jnp.where(lane >= n_w, lane - n_w, lane)
            picks.append((lane.astype(F32) == plane).astype(F32))
        w_pick = jnp.concatenate(picks, axis=0).astype(BF16)
        for start in range(0, cells, wide_step):
            re, im = pl.ds(start, wide_step), pl.ds(cells + start, wide_step)
            s_re, s_im = dot(w_pick, wcat[:, re]), dot(w_pick, wcat[:, im])
            for j in range(block):
                p = lax.rem(me + c * block + j + 1, n)
                t_re, t_im = spread(tap[p, 0:cap, re]), spread(tap[p, 0:cap, im])
                w_re, w_im = s_re[j * span:(j + 1) * span], s_im[j * span:(j + 1) * span]
                wt[pl.ds(j * span, span), re] = (t_re * w_re - t_im * w_im).astype(BF16)
                wt[pl.ds(j * span, span), im] = (t_re * w_im + t_im * w_re).astype(BF16)
        result = dot(wt[...], mat[...]).astype(BF16)
        sbuf[pl.ds(c * block, block)] = result.reshape(block, span, LANES)
        for j in range(block):
            i = c * block + j + 1

            @pl.when(i < n)
            def _():
                predicted(i).start()
        return carry

    lax.fori_loop(0, n // block, predict, 0)
    rbuf[me] = sbuf[n - 1]
    each(1, n, lambda i: arrival(rbuf, pred_sem, i).wait())

    total = n * cap
    wide[...] = rbuf[...].reshape(n * span, LANES).astype(F32)
    for t in range(ts):
        xbuf[:, pl.ds(t * LANES, LANES)] = wide[pl.ds(t, total, stride=ts), :].astype(BF16)
    moved = dot(move, xbuf[...])
    for t in range(ts):
        wide[pl.ds(t, total, stride=ts), :] = moved[:, t * LANES:(t + 1) * LANES]
    sbuf2[...] = wide[...].astype(BF16).reshape(n, span, LANES)
    each(1, n, lambda i: timed(i).start())
    rbuf2[me] = sbuf2[me]
    loads[9].wait()
    each(1, n, lambda i: arrival(rbuf2, time_sem, i).wait())

    wide[...] = rbuf2[...].reshape(n * span, LANES).astype(F32)
    for t in range(ts):
        at = pl.ds(t * LANES, LANES)
        out_ref[:, at] = (obs[:, at].astype(F32) - wide[pl.ds(t, total, stride=ts), :]).astype(BF16)

    def sent(i):
        request(i).wait_send()
        predicted(i).wait_send()
        timed(i).wait_send()

    each(1, n, sent)


def local(
    grid,
    patch_owner,
    patch_column,
    aperture_index,
    w_index,
    a_kernels,
    w_kernels,
    channel_response,
    time_owner,
    observed,
):
    n = lax.axis_size("bl")
    cap = observed.shape[0] // n
    capp = -(-cap // 8) * 8
    rows, ts = w_index.shape
    columns, width = grid.shape[1:]
    n_a, n_w = a_kernels.shape[0], w_kernels.shape[0]
    block = 4
    span = cap * ts
    vmem = pl.BlockSpec(memory_space=pltpu.VMEM)
    hbm = pl.BlockSpec(memory_space=pltpu.HBM)
    return pl.pallas_call(
        functools.partial(kernel, n, cap, capp, ts, block),
        out_shape=jax.ShapeDtypeStruct(observed.shape, BF16),
        in_specs=[hbm] * 10,
        out_specs=vmem,
        scratch_shapes=[
            pltpu.VMEM((columns, width), BF16),
            pltpu.VMEM((1, rows), jnp.int32),
            pltpu.VMEM((1, rows), jnp.int32),
            pltpu.VMEM((1, rows), jnp.int32),
            pltpu.VMEM((ts, rows), jnp.int32),
            pltpu.VMEM(a_kernels.shape, F32),
            pltpu.VMEM(w_kernels.shape, F32),
            pltpu.VMEM((2, channel_response.shape[2], width // 2), BF16),
            pltpu.VMEM((1, rows), jnp.int32),
            pltpu.VMEM(observed.shape, BF16),
            pltpu.VMEM((n, capp, LANES), F32),
            pltpu.VMEM((n, capp, LANES), F32),
            pltpu.VMEM((2 * n_a, width), BF16),
            pltpu.VMEM((2 * n_w, width), BF16),
            pltpu.VMEM((width, 2 * channel_response.shape[2]), BF16),
            pltpu.VMEM((n, capp, width), F32),
            pltpu.VMEM((block * span, width), BF16),
            pltpu.VMEM((n, span, LANES), BF16),
            pltpu.VMEM((n, span, LANES), BF16),
            pltpu.VMEM((n * span, LANES), F32),
            pltpu.VMEM((n * cap, ts * LANES), BF16),
            pltpu.VMEM((n, span, LANES), BF16),
            pltpu.VMEM((n, span, LANES), BF16),
            pltpu.SemaphoreType.DMA((10,)),
            pltpu.SemaphoreType.DMA((3, n)),
            pltpu.SemaphoreType.DMA((n,)),
            pltpu.SemaphoreType.DMA((n,)),
            pltpu.SemaphoreType.DMA((n,)),
        ],
        compiler_params=pltpu.CompilerParams(
            collective_id=0, has_side_effects=True, vmem_limit_bytes=64 * 1024 * 1024),
    )(grid.reshape(columns, width), patch_owner.T, patch_column[None], aperture_index[None], w_index.T,
      a_kernels, w_kernels, channel_response.transpose(0, 2, 1), time_owner.T, observed)


def solution(mesh):
    in_specs = (
        P(("groups", "bl"), None, None),
        P(("groups", "bl"), None),
        P(("groups", "bl")),
        P(("groups", "bl")),
        P(("groups", "bl"), None),
        P(),
        P(),
        P(None, None, "groups"),
        P(("groups", "bl"), None),
        P(("groups", "bl"), None),
    )
    out_specs = P(("groups", "bl"), None)
    return jax.shard_map(local, mesh=mesh, in_specs=in_specs, out_specs=out_specs, check_vma=False)
```

```python
import functools

import jax
import jax.numpy as jnp
from jax import lax
from jax.experimental import pallas as pl
from jax.experimental.pallas import tpu as pltpu
from jax.sharding import PartitionSpec as P

F32 = jnp.float32
BF16 = jnp.bfloat16
LANES = 128


def iota(shape, axis):
    return lax.broadcasted_iota(jnp.int32, shape, axis)


def dot(a, b):
    return jnp.dot(a, b, preferred_element_type=F32)


def dot_nt(a, b):
    return lax.dot_general(a, b, (((1,), (1,)), ((), ())), preferred_element_type=F32)


def owner_and_rank(owner, n):
    rows = owner.shape[1]
    hits = (iota((n, rows), 0) == owner).astype(F32)
    earlier = (iota((rows, rows), 0) < iota((rows, rows), 1)).astype(F32).astype(BF16)
    before = dot(hits.astype(BF16), earlier)
    return owner, jnp.sum(before * hits, axis=0, keepdims=True).astype(jnp.int32)


def one_hot_rows(slot, count):
    return (iota((count, slot.shape[1]), 0) == slot).astype(F32).astype(BF16)


def kernel(
    n, cap, capp, ts, block, halves,
    grid_hbm, powner_hbm, pcol_hbm, aper_hbm, windex_hbm, a_hbm, w_hbm, chan_hbm, towner_hbm, obs_hbm,
    out_ref,
    grid, powner, pcol, aper, windex, a_ref, w_ref, chan_ref, towner, obs, rs, rq, acat, wcat, mat, need, tap, wt, turn, sbuf, rbuf, wide, xbuf, sbuf2, rbuf2,
    local_sem, send_sem, req_sem, pred_sem, time_sem,
):
    me = lax.axis_index("bl")
    rows = windex.shape[1]
    cells = grid.shape[1] // 2
    columns = grid.shape[0]
    th = ts // halves
    span = cap * th
    total = n * cap

    def partner(k):
        there, bit = 0, 1
        while bit < n:
            there = there + bit * lax.rem(lax.div(me, bit) + lax.div(k, bit), 2)
            bit *= 2
        return there

    pairs = [(powner_hbm, powner), (pcol_hbm, pcol), (aper_hbm, aper), (windex_hbm, windex), (towner_hbm, towner),
             (a_hbm, a_ref), (w_hbm, w_ref), (chan_hbm, chan_ref), (grid_hbm, grid), (obs_hbm, obs)]
    loads = [pltpu.make_async_copy(source, target, local_sem.at[k]) for k, (source, target) in enumerate(pairs)]
    for load in loads:
        load.start()

    barrier = pltpu.get_barrier_semaphore()

    def greet(i, carry):
        pl.semaphore_signal(barrier, inc=1, device_id={"bl": lax.rem(me + i, n)},
                            device_id_type=pl.DeviceIdType.MESH)
        return carry

    lax.fori_loop(1, n, greet, 0)

    for load in loads[:5]:
        load.wait()
    p_owner, p_rank = owner_and_rank(powner[...], n)
    t_owner, t_rank = owner_and_rank(towner[...], n)
    column = pcol[...]
    place = iota((8, rows), 0)
    head = jnp.where(place == 0, jnp.right_shift(column, 5),
                     jnp.where(place == 1, jnp.bitwise_and(column, 31), jnp.where(place == 2, aper[...], 0)))
    data = jnp.concatenate([head.astype(F32), windex[...].astype(F32), jnp.zeros((LANES - 8 - ts, rows), F32)],
                           axis=0).astype(BF16)
    wanted = dot_nt(one_hot_rows(p_owner * capp + p_rank, n * capp), data)
    rs[...] = wanted.reshape(n, capp, LANES)

    pl.semaphore_wait(barrier, n - 1)

    def remote(source, target, sent_sem, there_sem, peer):
        return pltpu.make_async_remote_copy(
            src_ref=source, dst_ref=target, send_sem=sent_sem, recv_sem=there_sem,
            device_id={"bl": peer}, device_id_type=pl.DeviceIdType.MESH)

    def request(k):
        peer = partner(k)
        return remote(rs.at[peer], rq.at[me], send_sem.at[0, k], req_sem.at[me], peer)

    def predicted(h, k):
        return remote(sbuf.at[h, n - 1 - k], rbuf.at[h, me], send_sem.at[1 + h, k], pred_sem.at[h, me], partner(k))

    def timed(h, k):
        peer = partner(k)
        return remote(sbuf2.at[h, peer], rbuf2.at[h, me], send_sem.at[1 + halves + h, k], time_sem.at[h, me], peer)

    def arrival(buf, sem, k):
        sender = partner(k)
        return pltpu.make_async_copy(buf.at[sender], buf.at[sender], sem.at[sender])

    def each(act):
        def step(i, carry):
            act(n - 1 - i)
            return carry
        lax.fori_loop(0, n - 1, step, 0)

    each(lambda k: request(k).start())
    rq[me] = rs[me]

    for load in loads[5:8]:
        load.wait()
    for part in range(2):
        at = pl.ds(part * cells, cells)
        for source, table in ((a_ref, acat), (w_ref, wcat)):
            count = source.shape[0]
            value = source[:, part, :]
            high = value.astype(BF16)
            table[0:count, at] = high
            table[count:2 * count, at] = (value - high.astype(F32)).astype(BF16)
    real, imag = chan_ref[0], chan_ref[1]
    mat[0:cells] = jnp.concatenate([real, imag], axis=0).T
    mat[cells:2 * cells] = jnp.concatenate([-imag, real], axis=0).T
    move = dot_nt(one_hot_rows(t_owner * cap + t_rank, n * cap),
                  one_hot_rows(p_owner * cap + p_rank, n * cap)).astype(BF16)

    row = iota((total, 1), 0)
    turn_of = jnp.floor((row.astype(F32) + 0.5) / cap).astype(jnp.int32)
    source = jnp.bitwise_xor(n - 1 - turn_of, me) * capp + row - turn_of * cap
    compact = (iota((total, n * capp), 1) == source).astype(F32).astype(BF16)

    loads[8].wait()
    each(lambda k: arrival(rq, req_sem, k).wait())
    req = dot(compact, rq[...].reshape(n * capp, LANES).astype(BF16))
    need[...] = req

    n_a = a_ref.shape[0]
    wide_step = 256
    column = req[:, 0:1] * 32.0 + req[:, 1:2]
    pick = (iota((total, columns), 1).astype(F32) == column).astype(F32).astype(BF16)
    lane = iota((total, 2 * n_a), 1)
    lane = jnp.where(lane >= n_a, lane - n_a, lane)
    a_pick = (lane.astype(F32) == req[:, 2:3]).astype(F32).astype(BF16)
    for start in range(0, cells, wide_step):
        re, im = pl.ds(start, wide_step), pl.ds(cells + start, wide_step)
        p_re, p_im = dot(pick, grid[:, re]), dot(pick, grid[:, im])
        a_re, a_im = dot(a_pick, acat[:, re]), dot(a_pick, acat[:, im])
        tap[:, re] = p_re * a_re - p_im * a_im
        tap[:, im] = p_re * a_im + p_im * a_re

    n_w = w_ref.shape[0]
    lot = block * cap

    for h in range(halves):
        def predict(c, carry):
            at = pl.ds(pl.multiple_of(c * lot, 16), lot)
            plane = need[at, :]
            lane = iota((lot, 2 * n_w), 1)
            lane = jnp.where(lane >= n_w, lane - n_w, lane).astype(F32)
            w_pick = jnp.concatenate(
                [(lane == plane[:, 8 + h * th + t:9 + h * th + t]).astype(F32) for t in range(th)], axis=0).astype(BF16)
            for start in range(0, cells, wide_step):
                re, im = pl.ds(start, wide_step), pl.ds(cells + start, wide_step)
                s_re, s_im = dot(w_pick, wcat[:, re]), dot(w_pick, wcat[:, im])
                t_re, t_im = tap[at, re], tap[at, im]
                for t in range(th):
                    w_re, w_im = s_re[t * lot:(t + 1) * lot], s_im[t * lot:(t + 1) * lot]
                    wt[pl.ds(t * lot, lot), re] = (t_re * w_re - t_im * w_im).astype(BF16)
                    wt[pl.ds(t * lot, lot), im] = (t_re * w_im + t_im * w_re).astype(BF16)
            result = dot(wt[...], mat[...])
            for t in range(th):
                turn[pl.ds(t, lot, stride=th), :] = result[t * lot:(t + 1) * lot]
            sbuf[h, pl.ds(c * block, block)] = turn[...].astype(BF16).reshape(block, span, LANES)
            for j in range(block):
                k = n - 1 - (c * block + j)

                @pl.when(k > 0)
                def _():
                    predicted(h, k).start()
            return carry

        lax.fori_loop(0, n // block, predict, 0)
        rbuf[h, me] = sbuf[h, n - 1]

    for h in range(halves):
        each(lambda k: arrival(rbuf.at[h], pred_sem.at[h], k).wait())
        wide[...] = rbuf[h].reshape(n * span, LANES).astype(F32)
        for t in range(th):
            xbuf[:, pl.ds(t * LANES, LANES)] = wide[pl.ds(t, total, stride=th), :].astype(BF16)
        moved = dot(move, xbuf[...])
        for t in range(th):
            wide[pl.ds(t, total, stride=th), :] = moved[:, t * LANES:(t + 1) * LANES]
        sbuf2[h] = wide[...].astype(BF16).reshape(n, span, LANES)
        each(lambda k: timed(h, k).start())
        rbuf2[h, me] = sbuf2[h, me]
    loads[9].wait()
    for h in range(halves):
        each(lambda k: arrival(rbuf2.at[h], time_sem.at[h], k).wait())
        wide[...] = rbuf2[h].reshape(n * span, LANES).astype(F32)
        for t in range(th):
            at = pl.ds((h * th + t) * LANES, LANES)
            out_ref[:, at] = (obs[:, at].astype(F32) - wide[pl.ds(t, total, stride=th), :]).astype(BF16)

    def sent(k):
        request(k).wait_send()
        for h in range(halves):
            predicted(h, k).wait_send()
            timed(h, k).wait_send()

    each(sent)


def local(
    grid,
    patch_owner,
    patch_column,
    aperture_index,
    w_index,
    a_kernels,
    w_kernels,
    channel_response,
    time_owner,
    observed,
):
    n = lax.axis_size("bl")
    cap = observed.shape[0] // n
    capp = -(-cap // 8) * 8
    rows, ts = w_index.shape
    columns, width = grid.shape[1:]
    n_a, n_w = a_kernels.shape[0], w_kernels.shape[0]
    block = 4 if 4 * cap % 16 == 0 else 8
    halves = 2 if cap * ts // 2 % 16 == 0 else 1
    span = cap * ts // halves
    vmem = pl.BlockSpec(memory_space=pltpu.VMEM)
    hbm = pl.BlockSpec(memory_space=pltpu.HBM)
    return pl.pallas_call(
        functools.partial(kernel, n, cap, capp, ts, block, halves),
        out_shape=jax.ShapeDtypeStruct(observed.shape, BF16),
        in_specs=[hbm] * 10,
        out_specs=vmem,
        scratch_shapes=[
            pltpu.VMEM((columns, width), BF16),
            pltpu.VMEM((1, rows), jnp.int32),
            pltpu.VMEM((1, rows), jnp.int32),
            pltpu.VMEM((1, rows), jnp.int32),
            pltpu.VMEM((ts, rows), jnp.int32),
            pltpu.VMEM(a_kernels.shape, F32),
            pltpu.VMEM(w_kernels.shape, F32),
            pltpu.VMEM((2, channel_response.shape[2], width // 2), BF16),
            pltpu.VMEM((1, rows), jnp.int32),
            pltpu.VMEM(observed.shape, BF16),
            pltpu.VMEM((n, capp, LANES), F32),
            pltpu.VMEM((n, capp, LANES), F32),
            pltpu.VMEM((2 * n_a, width), BF16),
            pltpu.VMEM((2 * n_w, width), BF16),
            pltpu.VMEM((width, 2 * channel_response.shape[2]), BF16),
            pltpu.VMEM((n * cap, LANES), F32),
            pltpu.VMEM((n * cap, width), F32),
            pltpu.VMEM((block * span, width), BF16),
            pltpu.VMEM((block * span, LANES), F32),
            pltpu.VMEM((halves, n, span, LANES), BF16),
            pltpu.VMEM((halves, n, span, LANES), BF16),
            pltpu.VMEM((n * span, LANES), F32),
            pltpu.VMEM((n * cap, ts // halves * LANES), BF16),
            pltpu.VMEM((halves, n, span, LANES), BF16),
            pltpu.VMEM((halves, n, span, LANES), BF16),
            pltpu.SemaphoreType.DMA((10,)),
            pltpu.SemaphoreType.DMA((1 + 2 * halves, n)),
            pltpu.SemaphoreType.DMA((n,)),
            pltpu.SemaphoreType.DMA((halves, n)),
            pltpu.SemaphoreType.DMA((halves, n)),
        ],
        compiler_params=pltpu.CompilerParams(
            collective_id=0, has_side_effects=True, vmem_limit_bytes=64 * 1024 * 1024),
    )(grid.reshape(columns, width), patch_owner.T, patch_column[None], aperture_index[None], w_index.T,
      a_kernels, w_kernels, channel_response.transpose(0, 2, 1), time_owner.T, observed)


def solution(mesh):
    in_specs = (
        P(("groups", "bl"), None, None),
        P(("groups", "bl"), None),
        P(("groups", "bl")),
        P(("groups", "bl")),
        P(("groups", "bl"), None),
        P(),
        P(),
        P(None, None, "groups"),
        P(("groups", "bl"), None),
        P(("groups", "bl"), None),
    )
    out_specs = P(("groups", "bl"), None)
    return jax.shard_map(local, mesh=mesh, in_specs=in_specs, out_specs=out_specs, check_vma=False)
```

```python
import functools

import jax
import jax.numpy as jnp
from jax import lax
from jax.experimental import pallas as pl
from jax.experimental.pallas import tpu as pltpu
from jax.sharding import PartitionSpec as P

F32 = jnp.float32
BF16 = jnp.bfloat16
LANES = 128


def iota(shape, axis):
    return lax.broadcasted_iota(jnp.int32, shape, axis)


def dot(a, b):
    return jnp.dot(a, b, preferred_element_type=F32)


def dot_nt(a, b):
    return lax.dot_general(a, b, (((1,), (1,)), ((), ())), preferred_element_type=F32)


def owner_and_rank(owner, n):
    rows = owner.shape[1]
    hits = (iota((n, rows), 0) == owner).astype(F32)
    earlier = (iota((rows, rows), 0) < iota((rows, rows), 1)).astype(F32).astype(BF16)
    before = dot(hits.astype(BF16), earlier)
    return owner, jnp.sum(before * hits, axis=0, keepdims=True).astype(jnp.int32)


def one_hot_rows(slot, count):
    return (iota((count, slot.shape[1]), 0) == slot).astype(F32).astype(BF16)


def kernel(
    n, cap, capp, ts, block, halves,
    grid_hbm, powner_hbm, pcol_hbm, aper_hbm, windex_hbm, a_hbm, w_hbm, chan_hbm, towner_hbm, obs_hbm,
    out_ref,
    grid, powner, pcol, aper, windex, a_ref, w_ref, chan_ref, towner, obs, rs, rq, acat, wcat, mat, need, tap, wt, turn, sbuf, rbuf, wide, xbuf, sbuf2, rbuf2,
    local_sem, send_sem, req_sem, pred_sem, time_sem,
):
    me = lax.axis_index("bl")
    rows = windex.shape[1]
    cells = grid.shape[1] // 2
    columns = grid.shape[0]
    th = ts // halves
    span = cap * th
    total = n * cap

    group = min(n, 16)
    flips, bit = [], 1
    while bit < n:
        flips.append(bit * (1 - 2 * lax.rem(lax.div(me, bit), 2)))
        bit *= 2

    def partner(high, low):
        there = me
        for place, flip in enumerate(flips):
            if isinstance(high, int):
                if (high + low) >> place & 1:
                    there = there + flip
            elif low >> place & 1:
                there = there + flip
            elif place >= 2:
                there = there + flip * lax.rem(lax.div(high, 1 << place), 2)
        return there

    pairs = [(powner_hbm, powner), (pcol_hbm, pcol), (aper_hbm, aper), (windex_hbm, windex), (towner_hbm, towner),
             (a_hbm, a_ref), (w_hbm, w_ref), (chan_hbm, chan_ref), (grid_hbm, grid), (obs_hbm, obs)]
    loads = [pltpu.make_async_copy(source, target, local_sem.at[k]) for k, (source, target) in enumerate(pairs)]
    for load in loads:
        load.start()

    barrier = pltpu.get_barrier_semaphore()

    def greet(i, carry):
        pl.semaphore_signal(barrier, inc=1, device_id={"bl": lax.rem(me + i, n)},
                            device_id_type=pl.DeviceIdType.MESH)
        return carry

    lax.fori_loop(1, n, greet, 0, unroll=n <= 16)

    for load in loads[:5]:
        load.wait()
    p_owner, p_rank = owner_and_rank(powner[...], n)
    t_owner, t_rank = owner_and_rank(towner[...], n)
    column = pcol[...]
    place = iota((8, rows), 0)
    head = jnp.where(place == 0, jnp.right_shift(column, 5),
                     jnp.where(place == 1, jnp.bitwise_and(column, 31), jnp.where(place == 2, aper[...], 0)))
    data = jnp.concatenate([head.astype(F32), windex[...].astype(F32), jnp.zeros((LANES - 8 - ts, rows), F32)],
                           axis=0).astype(BF16)
    wanted = dot_nt(one_hot_rows(p_owner * capp + p_rank, n * capp), data)
    rs[...] = wanted.astype(BF16).reshape(n, capp, LANES)

    pl.semaphore_wait(barrier, n - 1)

    def remote(source, target, sent_sem, there_sem, peer):
        return pltpu.make_async_remote_copy(
            src_ref=source, dst_ref=target, send_sem=sent_sem, recv_sem=there_sem,
            device_id={"bl": peer}, device_id_type=pl.DeviceIdType.MESH)

    def request(peer):
        remote(rs.at[peer], rq.at[me], send_sem.at[0], req_sem, peer).start()

    def predicted(h, index, peer):
        remote(sbuf.at[h, index], rbuf.at[h, me], send_sem.at[1 + h], pred_sem.at[h], peer).start()

    def timed(h, peer):
        remote(sbuf2.at[h, peer], rbuf2.at[h, me], send_sem.at[1 + halves + h], time_sem.at[h], peer).start()

    def all_of(buf, sem):
        part = buf.at[pl.ds(0, n - 1)]
        pltpu.make_async_copy(part, part, sem).wait()

    def each(act):
        def step(i, carry):
            high = n - group * (i + 1)
            for low in reversed(range(group)):
                act(partner(high, low))
            return carry
        if n > group:
            lax.fori_loop(0, n // group - 1, step, 0)
        for low in reversed(range(1, group)):
            act(partner(0, low))

    each(request)
    rq[me] = rs[me]

    for load in loads[5:8]:
        load.wait()
    for part in range(2):
        at = pl.ds(part * cells, cells)
        for source, table in ((a_ref, acat), (w_ref, wcat)):
            count = source.shape[0]
            value = source[:, part, :]
            high = value.astype(BF16)
            table[0:count, at] = high
            table[count:2 * count, at] = (value - high.astype(F32)).astype(BF16)
    real, imag = chan_ref[0], chan_ref[1]
    mat[0:cells] = jnp.concatenate([real, imag], axis=0).T
    mat[cells:2 * cells] = jnp.concatenate([-imag, real], axis=0).T
    move = dot_nt(one_hot_rows(t_owner * cap + t_rank, n * cap),
                  one_hot_rows(p_owner * cap + p_rank, n * cap)).astype(BF16)

    row = iota((total, 1), 0)
    turn_of = jnp.floor((row.astype(F32) + 0.5) / cap).astype(jnp.int32)
    source = jnp.bitwise_xor(n - 1 - turn_of, me) * capp + row - turn_of * cap
    compact = (iota((total, n * capp), 1) == source).astype(F32).astype(BF16)

    loads[8].wait()
    all_of(rq, req_sem)
    req = dot(compact, rq[...].reshape(n * capp, LANES))
    need[...] = req

    n_a = a_ref.shape[0]
    wide_step = 256
    column = req[:, 0:1] * 32.0 + req[:, 1:2]
    pick = (iota((total, columns), 1).astype(F32) == column).astype(F32).astype(BF16)
    lane = iota((total, 2 * n_a), 1)
    lane = jnp.where(lane >= n_a, lane - n_a, lane)
    a_pick = (lane.astype(F32) == req[:, 2:3]).astype(F32).astype(BF16)
    for start in range(0, cells, wide_step):
        re, im = pl.ds(start, wide_step), pl.ds(cells + start, wide_step)
        p_re, p_im = dot(pick, grid[:, re]), dot(pick, grid[:, im])
        a_re, a_im = dot(a_pick, acat[:, re]), dot(a_pick, acat[:, im])
        tap[:, re] = p_re * a_re - p_im * a_im
        tap[:, im] = p_re * a_im + p_im * a_re

    n_w = w_ref.shape[0]
    lot = block * cap

    for h in range(halves):
        def predict(c, carry):
            at = pl.ds(c * lot if isinstance(c, int) else pl.multiple_of(c * lot, 16), lot)
            plane = need[at, :]
            lane = iota((lot, 2 * n_w), 1)
            lane = jnp.where(lane >= n_w, lane - n_w, lane).astype(F32)
            w_pick = jnp.concatenate(
                [(lane == plane[:, 8 + h * th + t:9 + h * th + t]).astype(F32) for t in range(th)], axis=0).astype(BF16)
            for start in range(0, cells, wide_step):
                re, im = pl.ds(start, wide_step), pl.ds(cells + start, wide_step)
                s_re, s_im = dot(w_pick, wcat[:, re]), dot(w_pick, wcat[:, im])
                t_re, t_im = tap[at, re], tap[at, im]
                for t in range(th):
                    w_re, w_im = s_re[t * lot:(t + 1) * lot], s_im[t * lot:(t + 1) * lot]
                    wt[pl.ds(t * lot, lot), re] = (t_re * w_re - t_im * w_im).astype(BF16)
                    wt[pl.ds(t * lot, lot), im] = (t_re * w_im + t_im * w_re).astype(BF16)
            result = dot(wt[...], mat[...])
            for t in range(th):
                turn[pl.ds(t, lot, stride=th), :] = result[t * lot:(t + 1) * lot]
            sbuf[h, pl.ds(c * block, block)] = turn[...].astype(BF16).reshape(block, span, LANES)
            high = n - block * (c + 1)
            for j in range(block):
                if isinstance(c, int) and high + block - 1 - j == 0:
                    continue
                peer = partner(high, block - 1 - j)
                if isinstance(c, int) or j < block - 1:
                    predicted(h, c * block + j, peer)
                else:
                    @pl.when(c < n // block - 1)
                    def _():
                        predicted(h, c * block + j, peer)
            return carry

        if n // block <= 4:
            for c in range(n // block):
                predict(c, 0)
        else:
            lax.fori_loop(0, n // block, predict, 0)
        rbuf[h, me] = sbuf[h, n - 1]

    for h in range(halves):
        all_of(rbuf.at[h], pred_sem.at[h])
        wide[...] = rbuf[h].reshape(n * span, LANES).astype(F32)
        for t in range(th):
            xbuf[:, pl.ds(t * LANES, LANES)] = wide[pl.ds(t, total, stride=th), :].astype(BF16)
        moved = dot(move, xbuf[...])
        for t in range(th):
            wide[pl.ds(t, total, stride=th), :] = moved[:, t * LANES:(t + 1) * LANES]
        sbuf2[h] = wide[...].astype(BF16).reshape(n, span, LANES)
        each(functools.partial(timed, h))
        rbuf2[h, me] = sbuf2[h, me]
    loads[9].wait()
    for h in range(halves):
        all_of(rbuf2.at[h], time_sem.at[h])
        wide[...] = rbuf2[h].reshape(n * span, LANES).astype(F32)
        for t in range(th):
            at = pl.ds((h * th + t) * LANES, LANES)
            out_ref[:, at] = (obs[:, at].astype(F32) - wide[pl.ds(t, total, stride=th), :]).astype(BF16)

    all_of(rs, send_sem.at[0])
    for h in range(halves):
        all_of(sbuf.at[h], send_sem.at[1 + h])
        all_of(sbuf2.at[h], send_sem.at[1 + halves + h])


def local(
    grid,
    patch_owner,
    patch_column,
    aperture_index,
    w_index,
    a_kernels,
    w_kernels,
    channel_response,
    time_owner,
    observed,
):
    n = lax.axis_size("bl")
    cap = observed.shape[0] // n
    capp = -(-cap // 16) * 16
    rows, ts = w_index.shape
    columns, width = grid.shape[1:]
    n_a, n_w = a_kernels.shape[0], w_kernels.shape[0]
    block = 4 if 4 * cap % 16 == 0 else 8
    halves = 2 if cap * ts // 2 % 16 == 0 else 1
    span = cap * ts // halves
    vmem = pl.BlockSpec(memory_space=pltpu.VMEM)
    hbm = pl.BlockSpec(memory_space=pltpu.HBM)
    return pl.pallas_call(
        functools.partial(kernel, n, cap, capp, ts, block, halves),
        out_shape=jax.ShapeDtypeStruct(observed.shape, BF16),
        in_specs=[hbm] * 10,
        out_specs=vmem,
        scratch_shapes=[
            pltpu.VMEM((columns, width), BF16),
            pltpu.VMEM((1, rows), jnp.int32),
            pltpu.VMEM((1, rows), jnp.int32),
            pltpu.VMEM((1, rows), jnp.int32),
            pltpu.VMEM((ts, rows), jnp.int32),
            pltpu.VMEM(a_kernels.shape, F32),
            pltpu.VMEM(w_kernels.shape, F32),
            pltpu.VMEM((2, channel_response.shape[2], width // 2), BF16),
            pltpu.VMEM((1, rows), jnp.int32),
            pltpu.VMEM(observed.shape, BF16),
            pltpu.VMEM((n, capp, LANES), BF16),
            pltpu.VMEM((n, capp, LANES), BF16),
            pltpu.VMEM((2 * n_a, width), BF16),
            pltpu.VMEM((2 * n_w, width), BF16),
            pltpu.VMEM((width, 2 * channel_response.shape[2]), BF16),
            pltpu.VMEM((n * cap, LANES), F32),
            pltpu.VMEM((n * cap, width), F32),
            pltpu.VMEM((block * span, width), BF16),
            pltpu.VMEM((block * span, LANES), F32),
            pltpu.VMEM((halves, n, span, LANES), BF16),
            pltpu.VMEM((halves, n, span, LANES), BF16),
            pltpu.VMEM((n * span, LANES), F32),
            pltpu.VMEM((n * cap, ts // halves * LANES), BF16),
            pltpu.VMEM((halves, n, span, LANES), BF16),
            pltpu.VMEM((halves, n, span, LANES), BF16),
            pltpu.SemaphoreType.DMA((10,)),
            pltpu.SemaphoreType.DMA((1 + 2 * halves,)),
            pltpu.SemaphoreType.DMA,
            pltpu.SemaphoreType.DMA((halves,)),
            pltpu.SemaphoreType.DMA((halves,)),
        ],
        compiler_params=pltpu.CompilerParams(
            collective_id=0, has_side_effects=True, vmem_limit_bytes=64 * 1024 * 1024),
    )(grid.reshape(columns, width), patch_owner.T, patch_column[None], aperture_index[None], w_index.T,
      a_kernels, w_kernels, channel_response.transpose(0, 2, 1), time_owner.T, observed)


def solution(mesh):
    in_specs = (
        P(("groups", "bl"), None, None),
        P(("groups", "bl"), None),
        P(("groups", "bl")),
        P(("groups", "bl")),
        P(("groups", "bl"), None),
        P(),
        P(),
        P(None, None, "groups"),
        P(("groups", "bl"), None),
        P(("groups", "bl"), None),
    )
    out_specs = P(("groups", "bl"), None)
    return jax.shard_map(local, mesh=mesh, in_specs=in_specs, out_specs=out_specs, check_vma=False)
```

```python
import functools

import jax
import jax.numpy as jnp
from jax import lax
from jax.experimental import pallas as pl
from jax.experimental.pallas import tpu as pltpu
from jax.sharding import PartitionSpec as P

F32 = jnp.float32
BF16 = jnp.bfloat16
LANES = 128


def iota(shape, axis):
    return lax.broadcasted_iota(jnp.int32, shape, axis)


def dot(a, b):
    return jnp.dot(a, b, preferred_element_type=F32)


def dot_nt(a, b):
    return lax.dot_general(a, b, (((1,), (1,)), ((), ())), preferred_element_type=F32)


def owner_and_rank(owner, n):
    rows = owner.shape[1]
    hits = (iota((n, rows), 0) == owner).astype(F32)
    earlier = (iota((rows, rows), 0) < iota((rows, rows), 1)).astype(F32).astype(BF16)
    before = dot(hits.astype(BF16), earlier)
    return owner, jnp.sum(before * hits, axis=0, keepdims=True).astype(jnp.int32)


def one_hot_rows(slot, count):
    return (iota((count, slot.shape[1]), 0) == slot).astype(F32).astype(BF16)


def kernel(
    n, cap, capp, ts, block, halves,
    grid_hbm, powner_hbm, pcol_hbm, aper_hbm, windex_hbm, a_hbm, w_hbm, chan_hbm, towner_hbm, obs_hbm,
    out_ref,
    grid, powner, pcol, aper, windex, a_ref, w_ref, chan_ref, towner, obs, rs, rq, acat, wcat, mat, need, tap, wt, turn, sbuf, rbuf, wide, xbuf, sbuf2, rbuf2,
    local_sem, send_sem, req_sem, pred_sem, time_sem,
):
    me = lax.axis_index("bl")
    rows = windex.shape[1]
    cells = grid.shape[1] // 2
    columns = grid.shape[0]
    th = ts // halves
    span = cap * th
    total = n * cap

    group = min(n, 16)
    flips, bit = [], 1
    while bit < n:
        flips.append(bit * (1 - 2 * lax.rem(lax.div(me, bit), 2)))
        bit *= 2

    def partner(high, low):
        there = me
        for place, flip in enumerate(flips):
            if isinstance(high, int):
                if (high + low) >> place & 1:
                    there = there + flip
            elif low >> place & 1:
                there = there + flip
            elif place >= 2:
                there = there + flip * lax.rem(lax.div(high, 1 << place), 2)
        return there

    barrier = pltpu.get_barrier_semaphore()

    def greet(i, carry):
        pl.semaphore_signal(barrier, inc=1, device_id={"bl": lax.rem(me + i, n)},
                            device_id_type=pl.DeviceIdType.MESH)
        return carry

    lax.fori_loop(1, n, greet, 0, unroll=n <= 16)

    pairs = [(powner_hbm, powner), (pcol_hbm, pcol), (aper_hbm, aper), (windex_hbm, windex), (towner_hbm, towner),
             (a_hbm, a_ref), (w_hbm, w_ref), (chan_hbm, chan_ref), (grid_hbm, grid), (obs_hbm, obs)]
    loads = [pltpu.make_async_copy(source, target, local_sem.at[k]) for k, (source, target) in enumerate(pairs)]
    for load in loads:
        load.start()

    for load in loads[:5]:
        load.wait()
    p_owner, p_rank = owner_and_rank(powner[...], n)
    t_owner, t_rank = owner_and_rank(towner[...], n)
    column = pcol[...]
    place = iota((8, rows), 0)
    head = jnp.where(place == 0, jnp.right_shift(column, 5),
                     jnp.where(place == 1, jnp.bitwise_and(column, 31), jnp.where(place == 2, aper[...], 0)))
    data = jnp.concatenate([head.astype(F32), windex[...].astype(F32), jnp.zeros((LANES - 8 - ts, rows), F32)],
                           axis=0).astype(BF16)
    wanted = dot_nt(one_hot_rows(p_owner * capp + p_rank, n * capp), data)
    rs[...] = wanted.astype(BF16).reshape(n, capp, LANES)

    pl.semaphore_wait(barrier, n - 1)

    def remote(source, target, sent_sem, there_sem, peer):
        return pltpu.make_async_remote_copy(
            src_ref=source, dst_ref=target, send_sem=sent_sem, recv_sem=there_sem,
            device_id={"bl": peer}, device_id_type=pl.DeviceIdType.MESH)

    def request(peer):
        remote(rs.at[peer], rq.at[me], send_sem.at[0], req_sem, peer).start()

    def predicted(h, index, peer):
        remote(sbuf.at[h, index], rbuf.at[h, me], send_sem.at[1 + h], pred_sem.at[h], peer).start()

    def timed(h, peer):
        remote(sbuf2.at[h, peer], rbuf2.at[h, me], send_sem.at[1 + halves + h], time_sem.at[h], peer).start()

    def all_of(buf, sem):
        part = buf.at[pl.ds(0, n - 1)]
        pltpu.make_async_copy(part, part, sem).wait()

    def each(act):
        def step(i, carry):
            high = n - group * (i + 1)
            for low in reversed(range(group)):
                act(partner(high, low))
            return carry
        if n > group:
            lax.fori_loop(0, n // group - 1, step, 0)
        for low in reversed(range(1, group)):
            act(partner(0, low))

    each(request)
    rq[me] = rs[me]

    for load in loads[5:8]:
        load.wait()
    for part in range(2):
        at = pl.ds(part * cells, cells)
        for source, table in ((a_ref, acat), (w_ref, wcat)):
            count = source.shape[0]
            value = source[:, part, :]
            high = value.astype(BF16)
            table[0:count, at] = high
            table[count:2 * count, at] = (value - high.astype(F32)).astype(BF16)
    real, imag = chan_ref[0], chan_ref[1]
    mat[0:cells] = jnp.concatenate([real, imag], axis=0).T
    mat[cells:2 * cells] = jnp.concatenate([-imag, real], axis=0).T
    move = dot_nt(one_hot_rows(t_owner * cap + t_rank, n * cap),
                  one_hot_rows(p_owner * cap + p_rank, n * cap)).astype(BF16)

    row = iota((total, 1), 0)
    turn_of = jnp.floor((row.astype(F32) + 0.5) / cap).astype(jnp.int32)
    source = jnp.bitwise_xor(n - 1 - turn_of, me) * capp + row - turn_of * cap
    compact = (iota((total, n * capp), 1) == source).astype(F32).astype(BF16)

    loads[8].wait()
    all_of(rq, req_sem)
    req = dot(compact, rq[...].reshape(n * capp, LANES))
    need[...] = req

    n_a = a_ref.shape[0]
    wide_step = 256

    def taper(first, count):
        at = pl.ds(first, count)
        mine = need[at, :]
        column = mine[:, 0:1] * 32.0 + mine[:, 1:2]
        pick = (iota((count, columns), 1).astype(F32) == column).astype(F32).astype(BF16)
        lane = iota((count, 2 * n_a), 1)
        lane = jnp.where(lane >= n_a, lane - n_a, lane)
        a_pick = (lane.astype(F32) == mine[:, 2:3]).astype(F32).astype(BF16)
        for start in range(0, cells, wide_step):
            re, im = pl.ds(start, wide_step), pl.ds(cells + start, wide_step)
            p_re, p_im = dot(pick, grid[:, re]), dot(pick, grid[:, im])
            a_re, a_im = dot(a_pick, acat[:, re]), dot(a_pick, acat[:, im])
            tap[at, re] = p_re * a_re - p_im * a_im
            tap[at, im] = p_re * a_im + p_im * a_re

    n_w = w_ref.shape[0]
    lot = block * cap
    run = 2

    for h in range(halves):
        def predict(c, carry):
            at = pl.ds(c * lot if isinstance(c, int) else pl.multiple_of(c * lot, 16), lot)
            plane = need[at, :]
            lane = iota((lot, 2 * n_w), 1)
            lane = jnp.where(lane >= n_w, lane - n_w, lane).astype(F32)
            w_pick = jnp.concatenate(
                [(lane == plane[:, 8 + h * th + t:9 + h * th + t]).astype(F32) for t in range(th)], axis=0).astype(BF16)
            for start in range(0, cells, wide_step):
                re, im = pl.ds(start, wide_step), pl.ds(cells + start, wide_step)
                s_re, s_im = dot(w_pick, wcat[:, re]), dot(w_pick, wcat[:, im])
                t_re, t_im = tap[at, re], tap[at, im]
                for t in range(th):
                    w_re, w_im = s_re[t * lot:(t + 1) * lot], s_im[t * lot:(t + 1) * lot]
                    wt[pl.ds(t * lot, lot), re] = (t_re * w_re - t_im * w_im).astype(BF16)
                    wt[pl.ds(t * lot, lot), im] = (t_re * w_im + t_im * w_re).astype(BF16)
            result = dot(wt[...], mat[...])
            for t in range(th):
                turn[pl.ds(t, lot, stride=th), :] = result[t * lot:(t + 1) * lot]
            sbuf[h, pl.ds(c * block, block)] = turn[...].astype(BF16).reshape(block, span, LANES)
            high = n - block * (c + 1)
            for j in range(block):
                if isinstance(c, int) and high + block - 1 - j == 0:
                    continue
                peer = partner(high, block - 1 - j)
                if isinstance(c, int) or j < block - 1:
                    predicted(h, c * block + j, peer)
                else:
                    @pl.when(c < n // block - 1)
                    def _():
                        predicted(h, c * block + j, peer)
            return carry

        if n // block <= 4:
            for c in range(n // block):
                if h == 0 and c % run == 0:
                    taper(c * lot, run * lot)
                predict(c, 0)
        else:
            if h == 0:
                taper(0, total)
            lax.fori_loop(0, n // block, predict, 0)
        rbuf[h, me] = sbuf[h, n - 1]

    for h in range(halves):
        all_of(rbuf.at[h], pred_sem.at[h])
        wide[...] = rbuf[h].reshape(n * span, LANES).astype(F32)
        for t in range(th):
            xbuf[:, pl.ds(t * LANES, LANES)] = wide[pl.ds(t, total, stride=th), :].astype(BF16)
        moved = dot(move, xbuf[...])
        for t in range(th):
            wide[pl.ds(t, total, stride=th), :] = moved[:, t * LANES:(t + 1) * LANES]
        sbuf2[h] = wide[...].astype(BF16).reshape(n, span, LANES)
        each(functools.partial(timed, h))
        rbuf2[h, me] = sbuf2[h, me]
    loads[9].wait()
    for h in range(halves):
        all_of(rbuf2.at[h], time_sem.at[h])
        wide[...] = rbuf2[h].reshape(n * span, LANES).astype(F32)
        for t in range(th):
            at = pl.ds((h * th + t) * LANES, LANES)
            out_ref[:, at] = (obs[:, at].astype(F32) - wide[pl.ds(t, total, stride=th), :]).astype(BF16)

    all_of(rs, send_sem.at[0])
    for h in range(halves):
        all_of(sbuf.at[h], send_sem.at[1 + h])
        all_of(sbuf2.at[h], send_sem.at[1 + halves + h])


def local(
    grid,
    patch_owner,
    patch_column,
    aperture_index,
    w_index,
    a_kernels,
    w_kernels,
    channel_response,
    time_owner,
    observed,
):
    n = lax.axis_size("bl")
    cap = observed.shape[0] // n
    capp = -(-cap // 16) * 16
    rows, ts = w_index.shape
    columns, width = grid.shape[1:]
    n_a, n_w = a_kernels.shape[0], w_kernels.shape[0]
    block = 4 if 4 * cap % 16 == 0 else 8
    halves = 2 if cap * ts // 2 % 16 == 0 else 1
    span = cap * ts // halves
    vmem = pl.BlockSpec(memory_space=pltpu.VMEM)
    hbm = pl.BlockSpec(memory_space=pltpu.HBM)
    return pl.pallas_call(
        functools.partial(kernel, n, cap, capp, ts, block, halves),
        out_shape=jax.ShapeDtypeStruct(observed.shape, BF16),
        in_specs=[hbm] * 10,
        out_specs=vmem,
        scratch_shapes=[
            pltpu.VMEM((columns, width), BF16),
            pltpu.VMEM((1, rows), jnp.int32),
            pltpu.VMEM((1, rows), jnp.int32),
            pltpu.VMEM((1, rows), jnp.int32),
            pltpu.VMEM((ts, rows), jnp.int32),
            pltpu.VMEM(a_kernels.shape, F32),
            pltpu.VMEM(w_kernels.shape, F32),
            pltpu.VMEM((2, channel_response.shape[2], width // 2), BF16),
            pltpu.VMEM((1, rows), jnp.int32),
            pltpu.VMEM(observed.shape, BF16),
            pltpu.VMEM((n, capp, LANES), BF16),
            pltpu.VMEM((n, capp, LANES), BF16),
            pltpu.VMEM((2 * n_a, width), BF16),
            pltpu.VMEM((2 * n_w, width), BF16),
            pltpu.VMEM((width, 2 * channel_response.shape[2]), BF16),
            pltpu.VMEM((n * cap, LANES), F32),
            pltpu.VMEM((n * cap, width), F32),
            pltpu.VMEM((block * span, width), BF16),
            pltpu.VMEM((block * span, LANES), F32),
            pltpu.VMEM((halves, n, span, LANES), BF16),
            pltpu.VMEM((halves, n, span, LANES), BF16),
            pltpu.VMEM((n * span, LANES), F32),
            pltpu.VMEM((n * cap, ts // halves * LANES), BF16),
            pltpu.VMEM((halves, n, span, LANES), BF16),
            pltpu.VMEM((halves, n, span, LANES), BF16),
            pltpu.SemaphoreType.DMA((10,)),
            pltpu.SemaphoreType.DMA((1 + 2 * halves,)),
            pltpu.SemaphoreType.DMA,
            pltpu.SemaphoreType.DMA((halves,)),
            pltpu.SemaphoreType.DMA((halves,)),
        ],
        compiler_params=pltpu.CompilerParams(
            collective_id=0, has_side_effects=True, vmem_limit_bytes=64 * 1024 * 1024),
    )(grid.reshape(columns, width), patch_owner.T, patch_column[None], aperture_index[None], w_index.T,
      a_kernels, w_kernels, channel_response.transpose(0, 2, 1), time_owner.T, observed)


def solution(mesh):
    in_specs = (
        P(("groups", "bl"), None, None),
        P(("groups", "bl"), None),
        P(("groups", "bl")),
        P(("groups", "bl")),
        P(("groups", "bl"), None),
        P(),
        P(),
        P(None, None, "groups"),
        P(("groups", "bl"), None),
        P(("groups", "bl"), None),
    )
    out_specs = P(("groups", "bl"), None)
    return jax.shard_map(local, mesh=mesh, in_specs=in_specs, out_specs=out_specs, check_vma=False)
```
